32 devices in a mesh: dp: 4 (over y, x), seq: 8 (over z, core).
Axes of the slice: x: 2, y: 2, z: 4, core: 2. Of those that a mesh axis runs over, the one named last changes fastest.
Arguments:
- hidden: bfloat16 [8, 1536, 3072], P('dp', 'seq'), may hold values from -6 to 6
- cotangent: bfloat16 [8, 1536, 1536], P('dp', 'seq'), may hold values from -6 to 6
- lengths: int32 [8], P('dp'), may hold values from 192 to 1536, as said below
- kernel: float32 [1536, 31], replicated, may hold values from -1 to 1
- conv_gain: float32 [1536], replicated, may hold values from 0.1 to 1.9
- w_out: bfloat16 [1536, 1536], replicated, may hold values from -0.15625 to 0.15625
Outputs:
- grad_hidden: bfloat16 [8, 1536, 3072], P('dp', 'seq')
- grad_w_out: float32 [1536, 1536], P(('dp', 'seq'))
- grad_kernel: float32 [1536, 31], P(('dp', 'seq'))
- grad_conv_gain: float32 [1536], P(('dp', 'seq'))
The draws below stay inside these ranges and needn't reach their ends.
Inputs may be any that keep to these rules, and one draw needn't show every extreme that they name: `lengths`: the first utterance of every group of 2 on one index of dp fills all 1536 frames.
All inputs are finite; a program needn't handle non-finite values.
Results may differ from the reference program's by a relative error of at most 0.0055.
Values may be sent and summed in bfloat16 or wider, within the bound.
A program may use at most 128 MiB of HBM per device.

```python
import math
import jax
import jax.numpy as jnp
from jax import lax

D = 1536
KW = 31
UTT = 2
BATCH = 8
LEN = 1536


def draw_lengths(key, part):
    drawn = jax.random.randint(key, (BATCH,), LEN // 8, LEN + 1, dtype=jnp.int32)
    leading = jnp.arange(BATCH, dtype=jnp.int32) % UTT == 0
    return jnp.where(leading, jnp.int32(LEN), drawn).astype(jnp.int32)


def strengthened(values, rng, source, target, shards_of, factor):
    def block_of(dim):
        return (jnp.arange(values.shape[dim]) // (values.shape[dim] // shards_of)).reshape((-1,) + (1,) * (values.ndim - 1 - dim))

    first = jax.random.permutation(rng, shards_of)[block_of(target)]
    far = (block_of(target) + shards_of // 2) % shards_of
    return jnp.where((block_of(source) == first) | (block_of(source) == far), factor * values, values)


def steps_of(own_key, extent, cuts, least, largest):
    gain, own = 1.0, jax.random.fold_in(own_key, 6)
    for position, parts in cuts:
        draws = jnp.exp(jax.random.uniform(jax.random.fold_in(own, position), (parts,), jnp.float32, least / len(cuts), largest / len(cuts)))
        gain = gain * jnp.repeat(draws, extent[position] // parts).reshape([-1 if axis == position else 1 for axis in range(len(extent))])
    return gain


def noise(rng, shape, spread, limit, split=(), kind=jnp.bfloat16):
    loudness = steps_of(rng, shape, split, -0.22, 0.18) if split else 1.0
    values = jax.random.normal(rng, shape, jnp.float32) * spread * loudness
    return jnp.minimum(jnp.maximum(values, -limit), limit).astype(kind)


def gaussian_with(own_key, extent, deviation, reach, cuts, heavy, kind=jnp.bfloat16):
    result = deviation * jax.random.normal(own_key, extent, jnp.float32)
    if cuts:
        result = result * steps_of(own_key, extent, cuts, -0.22, 0.18)
    return jnp.clip(strengthened(result, jax.random.fold_in(own_key, 3), *heavy), -reach, reach).astype(kind)


def setup_inputs(seed: int = 0) -> dict:
    keys = jax.random.split(jax.random.key(seed), 7)
    hidden = gaussian_with(keys[0], (BATCH, LEN, 2 * D), 1.0, 6.0, ((0, 4), (1, 8)), (1, 2, 8, 2.0))
    cotangent = noise(keys[1], (BATCH, LEN, D), 1.0, 6.0, ((0, 4), (1, 8)))
    lengths = draw_lengths(jax.random.fold_in(keys[6], 71), 0)
    kernel = noise(keys[3], (D, KW), KW ** -0.5, 1.0, (), jnp.float32)
    conv_gain = jnp.clip(1.0 + 0.18 * jax.random.normal(keys[4], (D,), jnp.float32), 0.1, 1.9)
    w_out = noise(keys[5], (D, D), D ** -0.5, 0.15625)
    return {"hidden": hidden, "cotangent": cotangent, "lengths": lengths, "kernel": kernel, "conv_gain": conv_gain, "w_out": w_out}


EPSILON = 1e-05

def normalize(values):
    centered = values - lax.optimization_barrier(jnp.mean(values, axis=-1, keepdims=True))
    inverse = lax.rsqrt(lax.optimization_barrier(jnp.mean(centered * centered, axis=-1, keepdims=True)) + EPSILON)
    return (centered * inverse, inverse)

def norm_backward(grad_hat, normed, inverse):
    return inverse * (grad_hat - lax.optimization_barrier(jnp.mean(grad_hat, axis=-1, keepdims=True)) - normed * lax.optimization_barrier(jnp.mean(grad_hat * normed, axis=-1, keepdims=True)))

def reference(hidden, cotangent, lengths, kernel, conv_gain, w_out):
    half_width = KW // 2

    def one_utterance(totals, pieces):
        sample, upstream, length = pieces
        valid_rows = (jnp.arange(LEN, dtype=jnp.int32) < length).astype(jnp.float32)[:, None]
        hidden_float = sample.astype(jnp.float32)
        linear = hidden_float[:, :D]
        gate_open = jax.nn.sigmoid(hidden_float[:, D:])
        glu_out = (linear * gate_open * valid_rows).astype(jnp.bfloat16)
        padded = jnp.pad(glu_out.astype(jnp.float32), ((half_width, half_width), (0, 0)))
        conv_out = padded[0:LEN] * kernel[:, 0]
        for offset in range(1, KW):
            conv_out = conv_out + padded[offset:offset + LEN] * kernel[:, offset]
        conv_hat, conv_inverse = normalize(conv_out)
        pre_act = conv_hat * conv_gain
        act_gate = jax.nn.sigmoid(pre_act)
        swished = (pre_act * act_gate).astype(jnp.bfloat16)
        grad_out = upstream * valid_rows.astype(jnp.bfloat16)
        term_out = jnp.dot(swished.T, grad_out, preferred_element_type=jnp.float32)
        grad_swish = jnp.dot(grad_out, w_out.T, preferred_element_type=jnp.float32)
        grad_pre = grad_swish * act_gate * (1.0 + pre_act * (1.0 - act_gate))
        term_conv = lax.optimization_barrier(jnp.sum(grad_pre * conv_hat, axis=0))
        grad_rounded = lax.optimization_barrier(norm_backward(grad_pre * conv_gain, conv_hat, conv_inverse).astype(jnp.bfloat16))
        grad_conv = grad_rounded.astype(jnp.float32)
        grad_padded = jnp.pad(grad_conv, ((half_width, half_width), (0, 0)))
        last_tap = KW - 1
        grad_glu = grad_padded[last_tap:last_tap + LEN] * kernel[:, 0]
        for offset in range(1, KW):
            grad_glu = grad_glu + grad_padded[last_tap - offset:last_tap - offset + LEN] * kernel[:, offset]
        term_kernel = jnp.stack([lax.optimization_barrier(jnp.sum(grad_conv * padded[offset:offset + LEN], axis=0)) for offset in range(KW)], axis=1)
        grad_glu = grad_glu * valid_rows
        grad_sample = jnp.concatenate([grad_glu * gate_open, grad_glu * linear * gate_open * (1.0 - gate_open)], axis=1).astype(jnp.bfloat16)
        terms = (term_out, term_kernel, term_conv)
        return (tuple((old + new for old, new in zip(totals, terms))), grad_sample)
    start_totals = (jnp.zeros((D, D), jnp.float32), jnp.zeros((D, KW), jnp.float32), jnp.zeros((D,), jnp.float32))
    totals, grad_hidden = lax.scan(one_utterance, start_totals, (hidden, cotangent, lengths))
    factor = 1.0 / math.sqrt(BATCH * LEN)
    return (grad_hidden, totals[0] * factor, totals[1] * factor, totals[2] * factor)
```

```python
import functools
import math

import jax
import jax.numpy as jnp
from jax import lax
from jax.experimental import pallas as pl
from jax.experimental.pallas import tpu as pltpu
from jax.sharding import PartitionSpec as P

EPSILON = 1e-05
LANES = 128
EDGE = 16
MESH = pl.DeviceIdType.MESH
VMEM_LIMIT = 56 * 2**20


def sigmoid(x):
    return jax.nn.sigmoid(x)


def chunk_of(frames):
    return 64 if frames % 64 == 0 else 32 if frames % 32 == 0 else 16


def forward_kernel(taps, lin_ref, gate_ref, left_ref, right_ref, valid_ref, taps_ref, gain_ref,
                   up_ref, swished_ref, grad_ref, term_ref, ext, conv):
    groups, frames, _ = lin_ref.shape
    blocks = conv.shape[0]
    width = blocks * LANES
    half = taps // 2
    block = pl.program_id(0)
    chunk = chunk_of(frames)
    for u in range(groups):
        gated = (
            lin_ref[u].astype(jnp.float32) * sigmoid(gate_ref[u].astype(jnp.float32)) * valid_ref[u]
        ).astype(jnp.bfloat16)
        ext[u, pl.ds(0, EDGE), :] = left_ref[u].astype(jnp.float32)
        ext[u, pl.ds(EDGE, frames), :] = gated.astype(jnp.float32)
        ext[u, pl.ds(EDGE + frames, EDGE), :] = right_ref[u].astype(jnp.float32)
        for start in range(0, frames, chunk):
            total = jnp.zeros((chunk, LANES), jnp.float32)
            for tap in range(taps):
                total = total + ext[u, pl.ds(start + tap + EDGE - half, chunk), :] * taps_ref[
                    pl.ds(tap, 1), :
                ]
            conv[block, pl.ds(u * frames + start, chunk), :] = total

    @pl.when(block == blocks - 1)
    def _():
        rows = EDGE
        term_ref[...] = jnp.zeros_like(term_ref)
        inverse_width = 1.0 / width

        def part(index, _):
            span = pl.ds(pl.multiple_of(index * rows, rows), rows)
            values = [conv[b, span, :] for b in range(blocks)]
            mean = jnp.sum(sum(values), axis=-1, keepdims=True) * inverse_width
            values = [v - mean for v in values]
            square = jnp.sum(sum(v * v for v in values), axis=-1, keepdims=True) * inverse_width
            inverse = lax.rsqrt(square + EPSILON)
            first = jnp.zeros((rows, LANES), jnp.float32)
            second = jnp.zeros((rows, LANES), jnp.float32)
            for b in range(blocks):
                lanes = pl.ds(b * LANES, LANES)
                gain = gain_ref[:, lanes]
                hat = values[b] * inverse
                pre = hat * gain
                gate = sigmoid(pre)
                swished_ref[span, lanes] = (pre * gate).astype(jnp.bfloat16)
                grad_pre = up_ref[span, lanes] * gate * (1.0 + pre * (1.0 - gate))
                product = grad_pre * hat
                term_ref[:, lanes] += product[:8] + product[8:]
                grad = grad_pre * gain
                first = first + grad
                second = second + grad * hat
                conv[b, span, :] = grad
                values[b] = hat
            mean_first = jnp.sum(first, axis=-1, keepdims=True) * inverse_width
            mean_second = jnp.sum(second, axis=-1, keepdims=True) * inverse_width
            for b in range(blocks):
                lanes = pl.ds(b * LANES, LANES)
                result = inverse * (conv[b, span, :] - mean_first - values[b] * mean_second)
                grad_ref[span, lanes] = result.astype(jnp.bfloat16)
            return 0

        lax.fori_loop(0, groups * frames // rows, part, 0)


def forward(hidden, left, right, valid, taps_rows, gain, upstream, taps):
    groups, frames, double = hidden.shape
    width = double // 2
    blocks = width // LANES
    rows = groups * frames
    whole = lambda shape: pl.BlockSpec(shape, lambda b: (0,) * len(shape))
    return pl.pallas_call(
        functools.partial(forward_kernel, taps),
        grid=(blocks,),
        in_specs=[
            pl.BlockSpec((groups, frames, LANES), lambda b: (0, 0, b)),
            pl.BlockSpec((groups, frames, LANES), lambda b: (0, 0, b + blocks)),
            pl.BlockSpec((groups, EDGE, LANES), lambda b: (0, 0, b)),
            pl.BlockSpec((groups, EDGE, LANES), lambda b: (0, 0, b)),
            whole((groups, frames, LANES)),
            pl.BlockSpec((taps_rows.shape[0], LANES), lambda b: (0, b)),
            whole((1, width)),
            whole((rows, width)),
        ],
        out_specs=[whole((rows, width)), whole((rows, width)), whole((8, width))],
        out_shape=[
            jax.ShapeDtypeStruct((rows, width), jnp.bfloat16),
            jax.ShapeDtypeStruct((rows, width), jnp.bfloat16),
            jax.ShapeDtypeStruct((8, width), jnp.float32),
        ],
        scratch_shapes=[
            pltpu.VMEM((groups, frames + 2 * EDGE, LANES), jnp.float32),
            pltpu.VMEM((blocks, rows, LANES), jnp.float32),
        ],
        compiler_params=pltpu.CompilerParams(vmem_limit_bytes=VMEM_LIMIT),
    )(hidden, hidden, left, right, valid, taps_rows, gain, upstream)


def orders_of(dp, seq):
    seq_bits, dp_bits = seq.bit_length() - 1, dp.bit_length() - 1
    others = list(range(seq_bits, seq_bits + dp_bits)) + list(range(1, seq_bits))
    turns = (0, 1, dp_bits)
    return [[0] + others[t:] + others[:t] for t in turns]


def place_of(index, order):
    place = 0
    for bit in order:
        place = place * 2 + (index >> bit) % 2
    return place


def backward_kernel(taps, dp, seq, reduce, factor, hidden_ref, grad_ref, swished_ref, out_ref, valid_ref,
                    taps_ref, hidden_grad_ref, sum_ref, term_ref, ext, gated, terms, halo, edge_send,
                    edge_recv, *scratch):
    groups, frames, double = hidden_ref.shape
    width = double // 2
    blocks = width // LANES
    half = taps // 2
    chunk = chunk_of(frames)
    my_dp, my_seq = lax.axis_index("dp"), lax.axis_index("seq")
    right = (my_dp, lax.rem(my_seq + 1, seq))
    left = (my_dp, lax.rem(my_seq + seq - 1, seq))
    seq_bits, dp_bits = seq.bit_length() - 1, dp.bit_length() - 1
    steps = seq_bits + dp_bits if reduce else 0

    def bit_of(bit):
        if bit < seq_bits:
            return lax.rem(my_seq // (1 << bit), 2)
        return lax.rem(my_dp // (1 << (bit - seq_bits)), 2)

    def partner_of(bit):
        turn = 1 - 2 * bit_of(bit)
        if bit < seq_bits:
            return (my_dp, my_seq + (1 << bit) * turn)
        return (my_dp + (1 << (bit - seq_bits)) * turn, my_seq)

    barrier = pltpu.get_barrier_semaphore()
    partners = [left, right] + [partner_of(b) for b in range(steps)]
    for device in partners:
        pl.semaphore_signal(barrier, inc=1, device_id=device, device_id_type=MESH)
    pl.semaphore_wait(barrier, len(partners))

    edges = []
    for u in range(groups):
        edges.append(pltpu.make_async_remote_copy(
            grad_ref.at[u, pl.ds(frames - EDGE, EDGE)], halo.at[0, u],
            edge_send.at[0, u], edge_recv.at[0, u], device_id=right, device_id_type=MESH))
        edges.append(pltpu.make_async_remote_copy(
            grad_ref.at[u, pl.ds(0, EDGE)], halo.at[1, u],
            edge_send.at[1, u], edge_recv.at[1, u], device_id=left, device_id_type=MESH))
    for copy in edges:
        copy.start()
    keep_left = jnp.where(my_seq == 0, 0.0, 1.0).astype(jnp.float32)
    keep_right = jnp.where(my_seq == seq - 1, 0.0, 1.0).astype(jnp.float32)

    def conv_block(block, _):
        lanes = pl.ds(pl.multiple_of(block * LANES, LANES), LANES)
        gate_lanes = pl.ds(pl.multiple_of(block * LANES + width, LANES), LANES)
        terms[...] = jnp.zeros_like(terms)

        def utterance(u, _):
            ext[pl.ds(0, EDGE), :] = halo[0, u, :, lanes].astype(jnp.float32) * keep_left
            ext[pl.ds(EDGE, frames), :] = grad_ref[u, :, lanes].astype(jnp.float32)
            ext[pl.ds(EDGE + frames, EDGE), :] = halo[1, u, :, lanes].astype(jnp.float32) * keep_right
            for start in range(0, frames, chunk):
                span = pl.ds(start, chunk)
                valid = valid_ref[u, span, :]
                linear = hidden_ref[u, span, lanes].astype(jnp.float32)
                gate = sigmoid(hidden_ref[u, span, gate_lanes].astype(jnp.float32))
                glu = (linear * gate * valid).astype(jnp.bfloat16).astype(jnp.float32)
                gated[...] = gate
                total = jnp.zeros((chunk, LANES), jnp.float32)
                for tap in range(taps):
                    moved = ext[pl.ds(start + EDGE + half - tap, chunk), :]
                    total = total + moved * taps_ref[pl.ds(tap, 1), lanes]
                    product = glu * moved
                    terms[tap] += sum(product[i : i + 8] for i in range(0, chunk, 8))
                gate = gated[...]
                opened = total * valid * gate
                linear = hidden_ref[u, span, lanes].astype(jnp.float32)
                hidden_grad_ref[u, span, lanes] = opened.astype(jnp.bfloat16)
                hidden_grad_ref[u, span, gate_lanes] = (
                    opened * linear * (1.0 - gate)
                ).astype(jnp.bfloat16)
            return 0

        lax.fori_loop(0, groups, utterance, 0)
        term_ref[:, lanes] = jnp.sum(terms[...], axis=1)
        return 0

    if not reduce:
        for copy in edges:
            copy.wait()
        lax.fori_loop(0, blocks, conv_block, 0)
        sum_ref[...] = jnp.zeros_like(sum_ref)
        return

    total, sending, landing, send_sem, recv_sem = scratch
    parts, count, depth, columns = total.shape
    orders = orders_of(dp, seq)
    offsets = [count - (count >> s) for s in range(steps)]
    bases = [0] * parts
    copies = [[None] * steps for _ in range(parts)]

    tile = LANES * depth // math.gcd(LANES, depth)
    for part in range(parts):
        for first in range(0, width, tile):
            product = lax.dot_general(
                swished_ref[:, pl.ds(first, tile)], out_ref[:, pl.ds(part * columns, columns)],
                (((0,), (0,)), ((), ())), preferred_element_type=jnp.float32)
            for i in range(tile // depth):
                place = place_of(first // depth + i, orders[part])
                total[part, place] = product[i * depth : (i + 1) * depth]

        launch(part, 0, steps, count, orders, bases, offsets, bit_of, partner_of, copies,
               total, sending, landing, send_sem, recv_sem)

    for copy in edges:
        copy.wait()
    share = [0] * (steps + 1)
    weights = [2, 4, 4, 2]
    done = 0
    for step in range(1, steps + 1):
        todo = min(blocks - done, weights[step - 1] * blocks // 12 if step < min(steps, 4) else blocks - done)
        if todo > 0:
            lax.fori_loop(done, done + todo, conv_block, 0)
            done += todo
        for part in range(parts):
            copies[part][step - 1].wait_recv()
            size = count >> step
            base, offset = bases[part], offsets[step - 1]
            if step < steps:
                def add(i, _, part=part, base=base, offset=offset):
                    total[part, base + i] += landing[part, offset + i].astype(jnp.float32)
                    return 0

                lax.fori_loop(0, size, add, 0)
                launch(part, step, steps, count, orders, bases, offsets, bit_of, partner_of, copies,
                       total, sending, landing, send_sem, recv_sem)
            else:
                sum_ref[:, pl.ds(part * columns, columns)] = factor * (
                    total[part, base] + landing[part, offset].astype(jnp.float32))
    for part in range(parts):
        for copy in copies[part]:
            copy.wait_send()


def launch(part, step, steps, count, orders, bases, offsets, bit_of, partner_of, copies,
           total, sending, landing, send_sem, recv_sem):
    bit = orders[part][step]
    size = count >> (step + 1)
    mine = bit_of(bit)
    away = bases[part] + (1 - mine) * size
    bases[part] = bases[part] + mine * size
    offset = offsets[step]

    def fill(i, _):
        sending[part, offset + i] = total[part, away + i].astype(jnp.bfloat16)
        return 0

    lax.fori_loop(0, size, fill, 0)
    copy = pltpu.make_async_remote_copy(
        sending.at[part, pl.ds(offset, size)], landing.at[part, pl.ds(offset, size)],
        send_sem.at[part, step], recv_sem.at[part, step],
        device_id=partner_of(bit), device_id_type=MESH)
    copy.start()
    copies[part][step] = copy


def backward(hidden, grad, swished, grad_out, valid, taps_rows, taps, dp, seq, reduce, factor):
    groups, frames, double = hidden.shape
    width = double // 2
    count = dp * seq
    depth = width // count
    parts = 3
    columns = width // parts
    steps = count.bit_length() - 1
    scratch = [
        pltpu.VMEM((frames + 2 * EDGE, LANES), jnp.float32),
        pltpu.VMEM((chunk_of(frames), LANES), jnp.float32),
        pltpu.VMEM((taps_rows.shape[0], 8, LANES), jnp.float32),
        pltpu.VMEM((2, groups, EDGE, width), jnp.bfloat16),
        pltpu.SemaphoreType.DMA((2, groups)),
        pltpu.SemaphoreType.DMA((2, groups)),
    ]
    if reduce:
        scratch += [
            pltpu.VMEM((parts, count, depth, columns), jnp.float32),
            pltpu.VMEM((parts, count, depth, columns), jnp.bfloat16),
            pltpu.VMEM((parts, count, depth, columns), jnp.bfloat16),
            pltpu.SemaphoreType.DMA((parts, steps)),
            pltpu.SemaphoreType.DMA((parts, steps)),
        ]
    vmem = pl.BlockSpec(memory_space=pltpu.VMEM)
    return pl.pallas_call(
        functools.partial(backward_kernel, taps, dp, seq, reduce, factor),
        in_specs=[vmem] * 6,
        out_specs=[vmem] * 3,
        out_shape=[
            jax.ShapeDtypeStruct(hidden.shape, jnp.bfloat16),
            jax.ShapeDtypeStruct((depth if reduce else 8, width), jnp.float32),
            jax.ShapeDtypeStruct((taps_rows.shape[0], width), jnp.float32),
        ],
        scratch_shapes=scratch,
        compiler_params=pltpu.CompilerParams(
            vmem_limit_bytes=VMEM_LIMIT, collective_id=0, has_side_effects=True),
    )(hidden, grad, swished, grad_out, valid, taps_rows)


def small_kernel(dp, seq, terms_ref, out_ref, landing, send_sem, recv_sem):
    count = dp * seq
    my_dp, my_seq = lax.axis_index("dp"), lax.axis_index("seq")
    me = my_dp * seq + my_seq

    def device(step):
        index = lax.rem(me + step, count)
        return index, (index // seq, lax.rem(index, seq))

    barrier = pltpu.get_barrier_semaphore()

    def greet(step, _):
        pl.semaphore_signal(barrier, inc=1, device_id=device(step)[1], device_id_type=MESH)
        return 0

    lax.fori_loop(1, count, greet, 0)
    pl.semaphore_wait(barrier, count - 1)

    def copy(step):
        index, target = device(step)
        return pltpu.make_async_remote_copy(
            terms_ref.at[index], landing.at[step], send_sem.at[step], recv_sem.at[step],
            device_id=target, device_id_type=MESH)

    def start(step, _):
        copy(step).start()
        return 0

    lax.fori_loop(1, count, start, 0)
    landing[0] = terms_ref[me]

    def finish(step, _):
        copy(step).wait()
        return 0

    lax.fori_loop(1, count, finish, 0)

    def add(step, total):
        return total + landing[step].astype(jnp.float32)

    out_ref[...] = lax.fori_loop(0, count, add, jnp.zeros(out_ref.shape, jnp.float32))


def small_sum(terms, dp, seq):
    count = dp * seq
    vmem = pl.BlockSpec(memory_space=pltpu.VMEM)
    return pl.pallas_call(
        functools.partial(small_kernel, dp, seq),
        in_specs=[vmem],
        out_specs=vmem,
        out_shape=jax.ShapeDtypeStruct(terms.shape[1:], jnp.float32),
        scratch_shapes=[
            pltpu.VMEM(terms.shape, jnp.bfloat16),
            pltpu.SemaphoreType.DMA((count,)),
            pltpu.SemaphoreType.DMA((count,)),
        ],
        compiler_params=pltpu.CompilerParams(collective_id=1, has_side_effects=True),
    )(terms)


def local(dp, seq, hidden, cotangent, lengths, kernel, conv_gain, w_out):
    groups, frames, double = hidden.shape
    width = double // 2
    taps = kernel.shape[1]
    rows = groups * frames
    count = dp * seq
    depth = width // count
    factor = 1.0 / math.sqrt(groups * dp * frames * seq)
    reduce = count & (count - 1) == 0 and depth % 16 == 0 and seq > 1 and dp > 1

    first = lax.axis_index("seq") * frames
    valid = (first + jnp.arange(frames, dtype=jnp.int32))[None, :] < lengths[:, None]
    valid_lanes = jnp.broadcast_to(valid.astype(jnp.float32)[:, :, None], (groups, frames, LANES))
    pad = -taps % 8
    taps_rows = jnp.pad(kernel.T, ((0, pad), (0, 0)))

    def gated_edge(start):
        cells = hidden[:, start : start + EDGE].astype(jnp.float32)
        here = valid[:, start : start + EDGE, None].astype(jnp.float32)
        return (cells[..., :width] * sigmoid(cells[..., width:]) * here).astype(jnp.bfloat16)

    left = lax.ppermute(gated_edge(frames - EDGE), "seq", [(i, i + 1) for i in range(seq - 1)])
    right = lax.ppermute(gated_edge(0), "seq", [(i + 1, i) for i in range(seq - 1)])

    grad_out = (cotangent * valid.astype(jnp.bfloat16)[:, :, None]).reshape(rows, width)
    upstream = lax.dot_general(
        grad_out, w_out, (((1,), (1,)), ((), ())), preferred_element_type=jnp.float32)

    swished, grad_conv, term_conv = forward(
        hidden, left, right, valid_lanes, taps_rows, conv_gain.reshape(1, width), upstream, taps)
    grad_hidden, sum_out, term_kernel = backward(
        hidden, grad_conv.reshape(groups, frames, width), swished, grad_out, valid_lanes, taps_rows,
        taps, dp, seq, reduce, factor)

    small = jnp.concatenate([term_kernel[:taps], jnp.sum(term_conv, axis=0, keepdims=True)], axis=0).T
    each = depth * (taps + 1)
    if reduce and each % LANES == 0:
        cells = small.astype(jnp.bfloat16).reshape(count, each // LANES, LANES)
        cells = jnp.pad(cells, ((0, 0), (0, -(each // LANES) % 16), (0, 0)))
        small = small_sum(cells, dp, seq)[: each // LANES].reshape(depth, taps + 1)
    else:
        small = lax.psum_scatter(small, ("dp", "seq"), scatter_dimension=0, tiled=True)
    if not reduce:
        term_out = lax.dot_general(
            swished, grad_out, (((0,), (0,)), ((), ())), preferred_element_type=jnp.float32)
        sum_out = factor * lax.psum_scatter(term_out, ("dp", "seq"), scatter_dimension=0, tiled=True)
    small = small * factor
    return (grad_hidden, sum_out, small[:, :taps], small[:, taps])


def solution(mesh):
    in_specs = (P("dp", "seq", None), P("dp", "seq", None), P("dp"), P(), P(), P())
    out_specs = (
        P("dp", "seq", None),
        P(("dp", "seq"), None),
        P(("dp", "seq"), None),
        P(("dp", "seq")),
    )
    return jax.shard_map(
        functools.partial(local, mesh.shape["dp"], mesh.shape["seq"]),
        mesh=mesh, in_specs=in_specs, out_specs=out_specs, check_vma=False)
```

```python
import functools
import math

import jax
import jax.numpy as jnp
from jax import lax
from jax.experimental import pallas as pl
from jax.experimental.pallas import tpu as pltpu
from jax.sharding import PartitionSpec as P

EPSILON = 1e-05
LANES = 128
EDGE = 16
MESH = pl.DeviceIdType.MESH
VMEM_LIMIT = 60 * 2**20


def sigmoid(x):
    return jax.nn.sigmoid(x)


def chunk_of(frames):
    return 64 if frames % 64 == 0 else 32 if frames % 32 == 0 else 16


def orders_of(dp, seq):
    seq_bits, dp_bits = seq.bit_length() - 1, dp.bit_length() - 1
    others = list(range(seq_bits, seq_bits + dp_bits)) + list(range(1, seq_bits))
    turns = (0, 1, dp_bits)
    return [[0] + others[t:] + others[:t] for t in turns]


def place_of(index, order):
    place = 0
    for bit in order:
        place = place * 2 + (index >> bit) % 2
    return place


def fused_kernel(taps, dp, seq, reduce, factor, plan, hidden_ref, cot_ref, w_ref, valid_ref, taps_ref, gain_ref,
                 hidden_grad_ref, sum_ref, small_ref, swished_ref, out_ref, w_here, upstream, conv, grad_ref,
                 term_conv, ext, gated, terms, rows_of_terms, edges, halo, w_sem, edge_send, edge_recv, *scratch):
    groups, frames, double = hidden_ref.shape
    width = double // 2
    blocks = width // LANES
    half = taps // 2
    chunk = chunk_of(frames)
    rows = groups * frames
    my_dp, my_seq = lax.axis_index("dp"), lax.axis_index("seq")
    right = (my_dp, lax.rem(my_seq + 1, seq))
    left = (my_dp, lax.rem(my_seq + seq - 1, seq))
    seq_bits, dp_bits = seq.bit_length() - 1, dp.bit_length() - 1
    steps = seq_bits + dp_bits if reduce else 0

    def bit_of(bit):
        if bit < seq_bits:
            return lax.rem(my_seq // (1 << bit), 2)
        return lax.rem(my_dp // (1 << (bit - seq_bits)), 2)

    def partner_of(bit):
        turn = 1 - 2 * bit_of(bit)
        if bit < seq_bits:
            return (my_dp, my_seq + (1 << bit) * turn)
        return (my_dp + (1 << (bit - seq_bits)) * turn, my_seq)

    def lanes_of(block, offset=0):
        return pl.ds(pl.multiple_of(block * LANES + offset, LANES), LANES)

    load_w = pltpu.make_async_copy(w_ref, w_here, w_sem)
    load_w.start()
    barrier = pltpu.get_barrier_semaphore()
    partners = [left, right] + [partner_of(b) for b in range(steps)]
    for device in partners:
        pl.semaphore_signal(barrier, inc=1, device_id=device, device_id_type=MESH)

    def gate_edges(block, _):
        lanes = lanes_of(block)
        for u in range(groups):
            for side, start in ((0, frames - EDGE), (1, 0)):
                span = pl.ds(start, EDGE)
                opened = sigmoid(hidden_ref[u, span, lanes_of(block, width)].astype(jnp.float32))
                cells = hidden_ref[u, span, lanes].astype(jnp.float32) * opened * valid_ref[u, span, :]
                edges[side, u, :, lanes] = cells.astype(jnp.bfloat16)
        return 0

    lax.fori_loop(0, blocks, gate_edges, 0)
    pl.semaphore_wait(barrier, len(partners))

    def exchange(turn, source):
        copies = []
        for side, device in ((0, right), (1, left)):
            for u in range(groups):
                copies.append(pltpu.make_async_remote_copy(
                    source(side, u), halo.at[turn, side, u], edge_send.at[turn, side, u],
                    edge_recv.at[turn, side, u], device_id=device, device_id_type=MESH))
        for copy in copies:
            copy.start()
        return copies

    first = exchange(0, lambda side, u: edges.at[side, u])
    keep_left = jnp.where(my_seq == 0, 0.0, 1.0).astype(jnp.float32)
    keep_right = jnp.where(my_seq == seq - 1, 0.0, 1.0).astype(jnp.float32)

    def mask(block, _):
        lanes = lanes_of(block)
        for u in range(groups):
            out_ref[pl.ds(u * frames, frames), lanes] = (
                cot_ref[u, :, lanes].astype(jnp.float32) * valid_ref[u]).astype(jnp.bfloat16)
        return 0

    lax.fori_loop(0, blocks, mask, 0)
    load_w.wait()
    wide = 2 * LANES if blocks % 2 == 0 else LANES

    def project(index, _):
        span = pl.ds(pl.multiple_of(index * wide, wide), wide)
        upstream[:, span] = lax.dot_general(
            out_ref[...], w_here[span, :], (((1,), (1,)), ((), ())), preferred_element_type=jnp.float32)
        return 0

    lax.fori_loop(0, width // wide, project, 0)
    for copy in first:
        copy.wait()

    def convolve(block, _):
        lanes = lanes_of(block)

        def utterance(u, _):
            opened = sigmoid(hidden_ref[u, :, lanes_of(block, width)].astype(jnp.float32))
            cells = hidden_ref[u, :, lanes].astype(jnp.float32) * opened * valid_ref[u]
            ext[pl.ds(0, EDGE), :] = halo[0, 0, u, :, lanes].astype(jnp.float32) * keep_left
            ext[pl.ds(EDGE, frames), :] = cells.astype(jnp.bfloat16).astype(jnp.float32)
            ext[pl.ds(EDGE + frames, EDGE), :] = halo[0, 1, u, :, lanes].astype(jnp.float32) * keep_right
            for start in range(0, frames, chunk):
                total = jnp.zeros((chunk, LANES), jnp.float32)
                for tap in range(taps):
                    total = total + ext[pl.ds(start + tap + EDGE - half, chunk), :] * taps_ref[
                        pl.ds(tap, 1), lanes]
                conv[block, u, pl.ds(start, chunk), :] = total
            return 0

        lax.fori_loop(0, groups, utterance, 0)
        return 0

    lax.fori_loop(0, blocks, convolve, 0)
    term_conv[...] = jnp.zeros_like(term_conv)
    inverse_width = 1.0 / width

    def normalise(index, _):
        u = index // (frames // EDGE)
        inner = pl.ds(pl.multiple_of(lax.rem(index, frames // EDGE) * EDGE, EDGE), EDGE)
        span = pl.ds(pl.multiple_of(index * EDGE, EDGE), EDGE)
        values = [conv[b, u, inner, :] for b in range(blocks)]
        mean = jnp.sum(sum(values), axis=-1, keepdims=True) * inverse_width
        values = [v - mean for v in values]
        square = jnp.sum(sum(v * v for v in values), axis=-1, keepdims=True) * inverse_width
        inverse = lax.rsqrt(square + EPSILON)
        one = jnp.zeros((EDGE, LANES), jnp.float32)
        two = jnp.zeros((EDGE, LANES), jnp.float32)
        for b in range(blocks):
            lanes = pl.ds(b * LANES, LANES)
            gain = gain_ref[:, lanes]
            hat = values[b] * inverse
            pre = hat * gain
            gate = sigmoid(pre)
            swished_ref[span, lanes] = (pre * gate).astype(jnp.bfloat16)
            grad_pre = upstream[span, lanes] * gate * (1.0 + pre * (1.0 - gate))
            product = grad_pre * hat
            term_conv[:, lanes] += product[:8] + product[8:]
            grad = grad_pre * gain
            one = one + grad
            two = two + grad * hat
            conv[b, u, inner, :] = grad
            values[b] = hat
        mean_one = jnp.sum(one, axis=-1, keepdims=True) * inverse_width
        mean_two = jnp.sum(two, axis=-1, keepdims=True) * inverse_width
        for b in range(blocks):
            lanes = pl.ds(b * LANES, LANES)
            result = inverse * (conv[b, u, inner, :] - mean_one - values[b] * mean_two)
            grad_ref[u, inner, lanes] = result.astype(jnp.bfloat16)
        return 0

    lax.fori_loop(0, rows // EDGE, normalise, 0)
    second = exchange(
        1, lambda side, u: grad_ref.at[u, pl.ds(0 if side else frames - EDGE, EDGE)])
    rows_of_terms[...] = jnp.zeros_like(rows_of_terms)
    rows_of_terms[pl.ds(taps, 1), :] = jnp.sum(term_conv[...], axis=0, keepdims=True)

    def conv_block(block, _):
        lanes = lanes_of(block)
        gate_lanes = lanes_of(block, width)
        terms[...] = jnp.zeros_like(terms)

        def utterance(u, _):
            ext[pl.ds(0, EDGE), :] = halo[1, 0, u, :, lanes].astype(jnp.float32) * keep_left
            ext[pl.ds(EDGE, frames), :] = grad_ref[u, :, lanes].astype(jnp.float32)
            ext[pl.ds(EDGE + frames, EDGE), :] = halo[1, 1, u, :, lanes].astype(jnp.float32) * keep_right
            for start in range(0, frames, chunk):
                span = pl.ds(start, chunk)
                valid = valid_ref[u, span, :]
                linear = hidden_ref[u, span, lanes].astype(jnp.float32)
                gate = sigmoid(hidden_ref[u, span, gate_lanes].astype(jnp.float32))
                glu = (linear * gate * valid).astype(jnp.bfloat16).astype(jnp.float32)
                gated[...] = gate
                total = jnp.zeros((chunk, LANES), jnp.float32)
                for tap in range(taps):
                    moved = ext[pl.ds(start + EDGE + half - tap, chunk), :]
                    total = total + moved * taps_ref[pl.ds(tap, 1), lanes]
                    product = glu * moved
                    terms[tap] += sum(product[i : i + 8] for i in range(0, chunk, 8))
                gate = gated[...]
                opened = total * valid_ref[u, span, :] * gate
                linear = hidden_ref[u, span, lanes].astype(jnp.float32)
                hidden_grad_ref[u, span, lanes] = opened.astype(jnp.bfloat16)
                hidden_grad_ref[u, span, gate_lanes] = (
                    opened * linear * (1.0 - gate)
                ).astype(jnp.bfloat16)
            return 0

        lax.fori_loop(0, groups, utterance, 0)
        rows_of_terms[pl.ds(0, taps), lanes] = jnp.sum(terms[...], axis=1)[:taps]
        return 0

    if not reduce:
        for copy in second:
            copy.wait()
        lax.fori_loop(0, blocks, conv_block, 0)
        sum_ref[...] = jnp.zeros_like(sum_ref)
        small_ref[...] = rows_of_terms[...]
        return

    total, sending, landing, tiny, tiny_sending, tiny_landing, send_sem, recv_sem = scratch
    parts, count, depth, columns = total.shape
    totals = [total.at[p] for p in range(parts)] + [tiny]
    sends = [sending.at[p] for p in range(parts)] + [tiny_sending]
    lands = [landing.at[p] for p in range(parts)] + [tiny_landing]
    orders = orders_of(dp, seq)
    orders.append(orders[0])
    bases = [0] * (parts + 1)
    copies = [[] for _ in range(parts + 1)]
    tile = LANES * depth // math.gcd(LANES, depth)

    def launch(part):
        step = len(copies[part])
        bit = orders[part][step]
        size = count >> (step + 1)
        mine = bit_of(bit)
        away = bases[part] + (1 - mine) * size
        bases[part] = bases[part] + mine * size
        offset = count - (count >> step)

        def fill(i, _):
            sends[part][offset + i] = totals[part][away + i].astype(jnp.bfloat16)
            return 0

        lax.fori_loop(0, size, fill, 0)
        copy = pltpu.make_async_remote_copy(
            sends[part].at[pl.ds(offset, size)], lands[part].at[pl.ds(offset, size)],
            send_sem.at[part, step], recv_sem.at[part, step],
            device_id=partner_of(bit), device_id_type=MESH)
        copy.start()
        copies[part].append(copy)

    def advance(part):
        step = len(copies[part])
        copies[part][step - 1].wait_recv()
        size = count >> step
        base, offset = bases[part], count - (count >> (step - 1))
        if step < steps:
            def add(i, _):
                totals[part][base + i] += lands[part][offset + i].astype(jnp.float32)
                return 0

            lax.fori_loop(0, size, add, 0)
            launch(part)
        else:
            value = factor * (totals[part][base] + lands[part][offset].astype(jnp.float32))
            if part < parts:
                sum_ref[:, pl.ds(part * columns, columns)] = value
            else:
                small_ref[...] = value

    for part in range(parts):
        for start in range(0, width, tile):
            product = lax.dot_general(
                swished_ref[:, pl.ds(start, tile)], out_ref[:, pl.ds(part * columns, columns)],
                (((0,), (0,)), ((), ())), preferred_element_type=jnp.float32)
            for i in range(tile // depth):
                total[part, place_of(start // depth + i, orders[part])] = product[
                    i * depth : (i + 1) * depth]
        launch(part)
    for copy in second:
        copy.wait()

    done = 0
    for number in range(len(plan)):
        upto = blocks if number == len(plan) - 1 else min(blocks, done + blocks * plan[number] // sum(plan))
        if upto > done:
            lax.fori_loop(done, upto, conv_block, 0)
            done = upto
        if number < len(plan) - 1:
            for part in range(parts):
                advance(part)
    for start in range(0, width, tile):
        turned = rows_of_terms[:, pl.ds(start, tile)].T
        for i in range(tile // depth):
            tiny[place_of(start // depth + i, orders[parts])] = turned[i * depth : (i + 1) * depth]
    launch(parts)
    left_over = [steps - len(copies[p]) + 1 for p in range(parts + 1)]
    while any(left_over):
        for part in [parts] + list(range(parts)):
            if left_over[part]:
                advance(part)
                left_over[part] -= 1
    for part in range(parts + 1):
        for copy in copies[part]:
            copy.wait_send()


def fused(hidden, cotangent, w_out, valid, taps_rows, gain, taps, dp, seq, reduce, factor):
    groups, frames, double = hidden.shape
    width = double // 2
    blocks = width // LANES
    rows = groups * frames
    count = dp * seq
    depth = width // count
    parts = 3
    columns = width // parts
    steps = count.bit_length() - 1
    small = -(-(taps + 1) // LANES) * LANES
    shared = [((rows, width), jnp.bfloat16)] * 2
    out_shape = [
        jax.ShapeDtypeStruct(hidden.shape, jnp.bfloat16),
        jax.ShapeDtypeStruct((depth if reduce else 8, width), jnp.float32),
        jax.ShapeDtypeStruct((depth, small) if reduce else (small, width), jnp.float32),
    ]
    scratch = [
        pltpu.VMEM((width, width), jnp.bfloat16),
        pltpu.VMEM((rows, width), jnp.float32),
        pltpu.VMEM((blocks, groups, frames, LANES), jnp.float32),
        pltpu.VMEM((groups, frames, width), jnp.bfloat16),
        pltpu.VMEM((8, width), jnp.float32),
        pltpu.VMEM((frames + 2 * EDGE, LANES), jnp.float32),
        pltpu.VMEM((chunk_of(frames), LANES), jnp.float32),
        pltpu.VMEM((taps_rows.shape[0], 8, LANES), jnp.float32),
        pltpu.VMEM((small, width), jnp.float32),
        pltpu.VMEM((2, groups, EDGE, width), jnp.bfloat16),
        pltpu.VMEM((2, 2, groups, EDGE, width), jnp.bfloat16),
        pltpu.SemaphoreType.DMA,
        pltpu.SemaphoreType.DMA((2, 2, groups)),
        pltpu.SemaphoreType.DMA((2, 2, groups)),
    ]
    if reduce:
        scratch = [pltpu.VMEM(*s) for s in shared] + scratch + [
            pltpu.VMEM((parts, count, depth, columns), jnp.float32),
            pltpu.VMEM((parts, count, depth, columns), jnp.bfloat16),
            pltpu.VMEM((parts, count, depth, columns), jnp.bfloat16),
            pltpu.VMEM((count, depth, small), jnp.float32),
            pltpu.VMEM((count, depth, small), jnp.bfloat16),
            pltpu.VMEM((count, depth, small), jnp.bfloat16),
            pltpu.SemaphoreType.DMA((parts + 1, steps)),
            pltpu.SemaphoreType.DMA((parts + 1, steps)),
        ]
    else:
        out_shape += [jax.ShapeDtypeStruct(*s) for s in shared]
    vmem = pl.BlockSpec(memory_space=pltpu.VMEM)
    plan = (3, 6, 3)
    return pl.pallas_call(
        functools.partial(fused_kernel, taps, dp, seq, reduce, factor, plan),
        in_specs=[vmem, vmem, pl.BlockSpec(memory_space=pl.ANY)] + [vmem] * 3,
        out_specs=[vmem] * len(out_shape),
        out_shape=out_shape,
        scratch_shapes=scratch,
        compiler_params=pltpu.CompilerParams(
            vmem_limit_bytes=VMEM_LIMIT, collective_id=0, has_side_effects=True),
    )(hidden, cotangent, w_out, valid, taps_rows, gain)


def local(dp, seq, hidden, cotangent, lengths, kernel, conv_gain, w_out):
    groups, frames, double = hidden.shape
    width = double // 2
    taps = kernel.shape[1]
    count = dp * seq
    depth = width // count
    factor = 1.0 / math.sqrt(groups * dp * frames * seq)
    reduce = count & (count - 1) == 0 and depth % 16 == 0 and seq > 1 and dp > 1

    first = lax.axis_index("seq") * frames
    valid = (first + jnp.arange(frames, dtype=jnp.int32))[None, :] < lengths[:, None]
    valid_lanes = jnp.broadcast_to(valid.astype(jnp.float32)[:, :, None], (groups, frames, LANES))
    taps_rows = jnp.pad(kernel.T, ((0, -taps % 8), (0, 0)))
    grad_hidden, sum_out, small, *rest = fused(
        hidden, cotangent, w_out, valid_lanes, taps_rows, conv_gain.reshape(1, width),
        taps, dp, seq, reduce, factor)
    if not reduce:
        swished, grad_out = rest
        term_out = lax.dot_general(
            swished, grad_out, (((0,), (0,)), ((), ())), preferred_element_type=jnp.float32)
        sum_out = factor * lax.psum_scatter(term_out, ("dp", "seq"), scatter_dimension=0, tiled=True)
        small = factor * lax.psum_scatter(
            small[: taps + 1].T, ("dp", "seq"), scatter_dimension=0, tiled=True)
    return (grad_hidden, sum_out, small[:, :taps], small[:, taps])


def solution(mesh):
    in_specs = (P("dp", "seq", None), P("dp", "seq", None), P("dp"), P(), P(), P())
    out_specs = (
        P("dp", "seq", None),
        P(("dp", "seq"), None),
        P(("dp", "seq"), None),
        P(("dp", "seq")),
    )
    return jax.shard_map(
        functools.partial(local, mesh.shape["dp"], mesh.shape["seq"]),
        mesh=mesh, in_specs=in_specs, out_specs=out_specs, check_vma=False)
```
